512 devices in a mesh: row: 16 (over x_hi, z), col: 32 (over y, x_lo, core).
Axes of the slice: x: 4 (x_hi: 2, x_lo: 2; x = x_hi * 2 + x_lo), y: 8, z: 8, core: 2. Of those that a mesh axis runs over, the one named last changes fastest.
Arguments:
- tokens: bfloat16 [256, 8192], P('col', 'row'), may hold values from -6 to 6
- upstream: bfloat16 [256, 8192], P('col', 'row'), may hold values from -6 to 6
- gate_pre: bfloat16 [256, 24576], P('row', 'col'), may hold values from -6 to 6
- up_pre: bfloat16 [256, 24576], P('row', 'col'), may hold values from -6 to 6
- w_gate: bfloat16 [8192, 24576], P('row', 'col'), may hold values from -0.0625 to 0.0625
- w_up: bfloat16 [8192, 24576], P('row', 'col'), may hold values from -0.0625 to 0.0625
- w_down: bfloat16 [24576, 8192], P('col', 'row'), may hold values from -0.0625 to 0.0625
Outputs:
- input_grad: bfloat16 [256, 8192], P('col', 'row')
- gate_grad: bfloat16 [8192, 24576], P('row', 'col')
- up_grad: bfloat16 [8192, 24576], P('row', 'col')
- down_grad: bfloat16 [24576, 8192], P('col', 'row')
The draws below stay inside these ranges and needn't reach their ends.
All inputs are finite; a program needn't handle non-finite values.
Results may differ from the reference program's by a relative error of at most 0.0049.
Values may be sent and summed in bfloat16 or wider, within the bound.
A program may use at most 64 MiB of HBM per device.

```python
import jax
import jax.numpy as jnp

D = 8192
FF = 24576
TOKENS = 256


def spiked(drawn, rng, source, target, parts, factor):
    owner, partner = [(jnp.arange(drawn.shape[axis_at]) // (drawn.shape[axis_at] // parts)).reshape([-1 if axis == axis_at else 1 for axis in range(drawn.ndim)]) for axis_at in (source, target)]
    chosen = jax.random.permutation(rng, parts)[partner]
    strong = (owner == chosen) | (owner == (partner + parts // 2) % parts)
    return jnp.where(strong, factor * drawn, drawn)


def block_scale(own_key, shape, split, low, largest):
    factor_of = 1.0
    for axis_at, shards_of in split:
        steps = jax.random.uniform(jax.random.fold_in(jax.random.fold_in(own_key, 6), axis_at), (shards_of,), jnp.float32, low / len(split), largest / len(split))
        factor_of = factor_of * jnp.repeat(jnp.exp(steps), shape[axis_at] // shards_of).reshape((-1,) + (1,) * (len(shape) - 1 - axis_at))
    return factor_of


def centred(key, dims, scale, limit, pieces=(), dtype=jnp.bfloat16):
    gain = block_scale(key, dims, pieces, -0.22, 0.18) if pieces else 1.0
    array = jax.random.normal(key, dims, jnp.float32) * scale * gain
    return jnp.minimum(jnp.maximum(array, -limit), limit).astype(dtype)


def heavy_noise(stream_key, shape, width, most, cuts, heavy, kind=jnp.bfloat16):
    result = width * jax.random.normal(stream_key, shape, jnp.float32)
    if cuts:
        result = result * block_scale(stream_key, shape, cuts, -0.22, 0.18)
    return jnp.clip(spiked(result, jax.random.fold_in(stream_key, 3), *heavy), -most, most).astype(kind)


def setup_inputs(seed: int = 0) -> dict:
    keys = jax.random.split(jax.random.key(seed), 8)
    return {
        "tokens": centred(keys[0], (TOKENS, D), 1.0, 6.0, ((0, 32), (1, 16))),
        "upstream": heavy_noise(keys[1], (TOKENS, D), 1.0, 6.0, ((0, 32), (1, 16)), (1, 0, 32, 2.75)),
        "gate_pre": centred(keys[2], (TOKENS, FF), 1.5, 6.0, ((0, 16), (1, 32))),
        "up_pre": heavy_noise(keys[3], (TOKENS, FF), 1.0, 6.0, ((0, 16), (1, 32)), (1, 0, 32, 2.75)),
        "w_gate": centred(keys[4], (D, FF), D ** -0.5, 0.0625, ((0, 16), (1, 32))),
        "w_up": centred(keys[5], (D, FF), D ** -0.5, 0.0625, ((0, 16), (1, 32))),
        "w_down": centred(keys[6], (FF, D), D ** -0.5, 0.0625, ((0, 32), (1, 16))),
    }


def reference(tokens, upstream, gate_pre, up_pre, w_gate, w_up, w_down):
    hidden_grad = jnp.dot(upstream, w_down.T, preferred_element_type=jnp.float32)
    gate_value = gate_pre.astype(jnp.float32)
    up_value = up_pre.astype(jnp.float32)
    sigmoid_gate = jax.nn.sigmoid(gate_value)
    activated = gate_value * sigmoid_gate
    hidden = (activated * up_value).astype(jnp.bfloat16)
    up_delta = (hidden_grad * activated).astype(jnp.bfloat16)
    slope = sigmoid_gate * (1.0 + gate_value * (1.0 - sigmoid_gate))
    gate_delta = (hidden_grad * up_value * slope).astype(jnp.bfloat16)
    input_grad = (jnp.dot(gate_delta, w_gate.T, preferred_element_type=jnp.float32)
                  + jnp.dot(up_delta, w_up.T, preferred_element_type=jnp.float32)).astype(jnp.bfloat16)
    grad_scale = float(TOKENS) ** -0.5
    gate_grad = (jnp.dot(tokens.T, gate_delta, preferred_element_type=jnp.float32) * grad_scale).astype(jnp.bfloat16)
    up_grad = (jnp.dot(tokens.T, up_delta, preferred_element_type=jnp.float32) * grad_scale).astype(jnp.bfloat16)
    down_grad = (jnp.dot(hidden.T, upstream, preferred_element_type=jnp.float32) * grad_scale).astype(jnp.bfloat16)
    return (input_grad, gate_grad, up_grad, down_grad)
```

```python
import functools

import jax
import jax.numpy as jnp
from jax import lax
from jax.experimental import pallas as pl
from jax.experimental.pallas import tpu as pltpu
from jax.sharding import PartitionSpec as P

MESH = pl.DeviceIdType.MESH
F32 = jnp.float32
BF16 = jnp.bfloat16
LAST = (((1,), (1,)), ((), ()))
FIRST = (((0,), (0,)), ((), ()))


def far_first(n):
    return sorted(range(1, n), key=lambda d: (-min(d, n - d), d))


def near_first(n):
    return sorted(range(1, n), key=lambda d: (min(d, n - d), d))


def exchange(
    n,
    ups, tok, gate, upre, w_gate, w_up, w_down,
    ig_out, gd_out, ud_out, hid_out, tok_out, ups_out,
    wg, wu, wd, ups_buf, tok_buf, gp_buf, up_buf, own_part, x_send, x_recv, z_send, z_recv,
    hg_buf, act, slope_up, ig_part, core_recv, xl_send, xl_recv, y_send, y_recv,
    local_sem, send_sem, ups_sem, tok_sem, gp_sem, up_sem, half_sem, quad_sem,
    xr_sem, zr_sem, hz_sem, hx_sem, ig_sem, ig_y_sem,
):
    row, col = lax.axis_index("row"), lax.axis_index("col")
    xh, z = row // n, lax.rem(row, n)
    y, q = col // 4, lax.rem(col, 4)
    xl, co = q // 2, lax.rem(q, 2)
    other = 1 - xh

    def z_peer(d):
        return (xh * n + lax.rem(z + d, n), col)

    def y_peer(d):
        return (row, lax.rem(y + d, n) * 4 + q)

    xh_peer = (other * n + z, col)
    xl_peer = (row, y * 4 + (1 - xl) * 2 + co)
    co_peer = (row, y * 4 + xl * 2 + (1 - co))

    sends = []

    def send(src, dst, sem, device):
        k = len(sends)
        copy = pltpu.make_async_remote_copy(
            src_ref=src, dst_ref=dst, send_sem=send_sem.at[k], recv_sem=sem,
            device_id=device, device_id_type=MESH,
        )
        copy.start()
        sends.append(copy)
        return copy

    locals_ = []

    def local(src, dst):
        copy = pltpu.make_async_copy(src, dst, local_sem.at[len(locals_)])
        copy.start()
        locals_.append(copy)
        return copy

    barrier = pltpu.get_barrier_semaphore()
    peers = [xh_peer, xl_peer, co_peer]
    for d in far_first(n):
        peers += [y_peer(d), z_peer(d)]
    for device in peers:
        pl.semaphore_signal(barrier, inc=1, device_id=device, device_id_type=MESH)
    own_ups = local(ups, ups_buf.at[q, y])
    own_gp = local(gate, gp_buf.at[row])
    own_up = local(upre, up_buf.at[row])
    own_wd = local(w_down, wd)
    own_tok = local(tok, tok_buf.at[q, y])
    own_wg = local(w_gate, wg)
    own_wu = local(w_up, wu)
    pl.semaphore_wait(barrier, len(peers))

    ups_y = {d: send(ups, ups_buf.at[q, y], ups_sem.at[d], y_peer(d)) for d in far_first(n)}
    gp_z, up_z = {}, {}
    for d in far_first(n):
        gp_z[d] = send(gate, gp_buf.at[row], gp_sem.at[d], z_peer(d))
        up_z[d] = send(upre, up_buf.at[row], up_sem.at[d], z_peer(d))
    tok_y = {d: send(tok, tok_buf.at[q, y], tok_sem.at[d], y_peer(d)) for d in far_first(n)}

    own_ups.wait()
    for d in near_first(n):
        ups_y[d].wait_recv()
    mine, theirs = ups_buf.at[q], ups_buf.at[(1 - xl) * 2 + co]
    ups_xl = send(mine, mine, quad_sem.at[0], xl_peer)
    ups_co = send(mine, mine, quad_sem.at[1], co_peer)
    ups_xl.wait_recv()
    ups_both = send(theirs, theirs, quad_sem.at[2], co_peer)
    own_wd.wait()
    ups_co.wait_recv()
    ups_both.wait_recv()

    def order_tokens(buf, out, first, count):
        @pl.loop(0, count)
        def _(k):
            rows = buf[:, first + k].astype(F32).reshape(32, buf.shape[-1])
            out[pl.ds(pl.multiple_of((first + k) * 32, 32), 32), :] = rows.astype(BF16)

    half = 16 * n
    near_rows = pl.ds(pl.multiple_of(xh * half, half), half)
    far_rows = pl.ds(pl.multiple_of(other * half, half), half)
    near_blocks, far_blocks = pl.ds(xh * n, n), pl.ds(other * n, n)

    order_tokens(ups_buf, ups_out, other * (n // 2), n // 2)
    part = lax.dot_general(ups_out[far_rows, :], wd[...], LAST, preferred_element_type=F32)
    x_send[...] = part.astype(BF16).reshape(x_send.shape)
    x_order = far_first(n) + [0]
    parts_x = {}
    for d in x_order:
        k = lax.rem(z + d, n)
        parts_x[d] = send(x_send.at[k], x_recv.at[k], xr_sem.at[d], xh_peer)
    order_tokens(ups_buf, ups_out, xh * (n // 2), n // 2)
    part = lax.dot_general(ups_out[near_rows, :], wd[...], LAST, preferred_element_type=F32)
    own_part[...] = part.reshape(own_part.shape)

    parts_z = {}
    for d in x_order:
        k = lax.rem(z + d, n)
        parts_x[d].wait_recv()
        total = own_part[k] + x_recv[k].astype(F32)
        if d:
            z_send[k] = total.astype(BF16)
            parts_z[d] = send(z_send.at[k], z_recv.at[d], zr_sem.at[d], z_peer(d))
        else:
            own_part[k] = total

    own_gp.wait()
    own_up.wait()
    for d in near_first(n):
        gp_z[d].wait_recv()
        up_z[d].wait_recv()
    gp_x = send(gp_buf.at[near_blocks], gp_buf.at[near_blocks], half_sem.at[0], xh_peer)
    up_x = send(up_buf.at[near_blocks], up_buf.at[near_blocks], half_sem.at[1], xh_peer)

    def activations(first):
        @pl.loop(0, n)
        def _(j):
            k = first + j
            g = gp_buf[k].astype(F32)
            u = up_buf[k].astype(F32)
            s = jax.nn.sigmoid(g)
            activated = g * s
            act[k] = activated
            slope_up[k] = u * (s * (1.0 + g * (1.0 - s)))
            hid_out[pl.ds(pl.multiple_of(k * 16, 16), 16), :] = (activated * u).astype(BF16)

    activations(xh * n)

    own_tok.wait()
    for d in near_first(n):
        tok_y[d].wait_recv()
    t_mine, t_theirs = tok_buf.at[q], tok_buf.at[(1 - xl) * 2 + co]
    tok_xl = send(t_mine, t_mine, quad_sem.at[3], xl_peer)
    tok_co = send(t_mine, t_mine, quad_sem.at[4], co_peer)

    total = own_part[z]
    for d in near_first(n):
        parts_z[d].wait_recv()
        total = total + z_recv[d].astype(F32)
    hg_buf[row] = total.astype(BF16)
    hg_mine = hg_buf.at[row]
    hg_z = {d: send(hg_mine, hg_mine, hz_sem.at[d], z_peer(d)) for d in far_first(n)}
    hg_x = [send(hg_mine, hg_mine, hx_sem.at[0], xh_peer)]

    gp_x.wait_recv()
    up_x.wait_recv()
    activations(other * n)
    tok_xl.wait_recv()
    tok_both = send(t_theirs, t_theirs, quad_sem.at[5], co_peer)
    own_wg.wait()
    own_wu.wait()

    for d in near_first(n):
        hg_z[d].wait_recv()
        block = hg_buf.at[xh * n + lax.rem(z - d + n, n)]
        hg_x.append(send(block, block, hx_sem.at[d], xh_peer))

    def deltas(first):
        @pl.loop(0, n)
        def _(j):
            k = first + j
            grad = hg_buf[k].astype(F32)
            rows = pl.ds(pl.multiple_of(k * 16, 16), 16)
            gd_out[rows, :] = (grad * slope_up[k]).astype(BF16)
            ud_out[rows, :] = (grad * act[k]).astype(BF16)

    def input_part(rows, blocks, sem):
        part = lax.dot_general(gd_out[rows, :], wg[...], LAST, preferred_element_type=F32)
        part = part + lax.dot_general(ud_out[rows, :], wu[...], LAST, preferred_element_type=F32)
        ig_part[blocks] = part.reshape(n, 2, 8, part.shape[-1])
        return send(ig_part.at[blocks, 1 - co], core_recv.at[blocks], sem, co_peer)

    def to_xl(first, sem):
        @pl.loop(0, n // 2)
        def _(j):
            k = 2 * (first + j) + 1 - xl
            xl_send[first + j] = (ig_part[k, co] + core_recv[k]).astype(BF16)

        blocks = pl.ds(first, n // 2)
        return send(xl_send.at[blocks], xl_recv.at[blocks], sem, xl_peer)

    deltas(xh * n)
    near_co = input_part(near_rows, near_blocks, ig_sem.at[0])
    for copy in hg_x:
        copy.wait_recv()
    deltas(other * n)
    near_co.wait_recv()
    near_xl = to_xl(xh * (n // 2), ig_sem.at[2])
    far_co = input_part(far_rows, far_blocks, ig_sem.at[1])
    far_co.wait_recv()
    far_xl = to_xl(other * (n // 2), ig_sem.at[3])

    def ig_block(k):
        return ig_part[2 * k + xl, co] + core_recv[2 * k + xl] + xl_recv[k].astype(F32)

    near_xl.wait_recv()
    far_xl.wait_recv()
    ig_y = {}
    for d in far_first(n):
        k = lax.rem(y + d, n)
        y_send[k] = ig_block(k).astype(BF16)
        ig_y[d] = send(y_send.at[k], y_recv.at[d], ig_y_sem.at[d], y_peer(d))
    total = ig_block(y)

    tok_co.wait_recv()
    tok_both.wait_recv()
    order_tokens(tok_buf, tok_out, 0, n)

    for d in near_first(n):
        ig_y[d].wait_recv()
        total = total + y_recv[d].astype(F32)
    ig_out[...] = total.astype(BF16)

    for copy in sends:
        copy.wait_send()


def weight_grads(scale, ig, gd, ud, hid, tok, ups, input_grad, gate_grad, up_grad, down_grad):
    def scaled(a, b):
        return (lax.dot_general(a, b, FIRST, preferred_element_type=F32) * scale).astype(BF16)

    input_grad[...] = ig[...]
    gate_grad[...] = scaled(tok[...], gd[...])
    up_grad[...] = scaled(tok[...], ud[...])
    down_grad[...] = scaled(hid[...], ups[...])


def on_device(n, tokens, upstream, gate_pre, up_pre, w_gate, w_up, w_down):
    d_block, f_block = w_gate.shape
    total = 32 * n
    blocks = 2 * n
    dma = pltpu.SemaphoreType.DMA
    hbm_spec = pl.BlockSpec(memory_space=pltpu.HBM)
    vmem_spec = pl.BlockSpec(memory_space=pltpu.VMEM)
    n_sends = 7 * (n - 1) + n + 1 + 2 + 6 + 4 + (n - 1) + 1
    ig, gd, ud, hid, tok, ups = pl.pallas_call(
        functools.partial(exchange, n),
        name="exchange",
        out_shape=(
            jax.ShapeDtypeStruct((8, d_block), BF16),
            jax.ShapeDtypeStruct((total, f_block), BF16),
            jax.ShapeDtypeStruct((total, f_block), BF16),
            jax.ShapeDtypeStruct((total, f_block), BF16),
            jax.ShapeDtypeStruct((total, d_block), BF16),
            jax.ShapeDtypeStruct((total, d_block), BF16),
        ),
        in_specs=[hbm_spec] * 7,
        out_specs=[vmem_spec] * 6,
        scratch_shapes=[
            pltpu.VMEM((d_block, f_block), BF16),
            pltpu.VMEM((d_block, f_block), BF16),
            pltpu.VMEM((f_block, d_block), BF16),
            pltpu.VMEM((4, n, 8, d_block), BF16),
            pltpu.VMEM((4, n, 8, d_block), BF16),
            pltpu.VMEM((blocks, 16, f_block), BF16),
            pltpu.VMEM((blocks, 16, f_block), BF16),
            pltpu.VMEM((n, 16, f_block), F32),
            pltpu.VMEM((n, 16, f_block), BF16),
            pltpu.VMEM((n, 16, f_block), BF16),
            pltpu.VMEM((n, 16, f_block), BF16),
            pltpu.VMEM((n, 16, f_block), BF16),
            pltpu.VMEM((blocks, 16, f_block), BF16),
            pltpu.VMEM((blocks, 16, f_block), F32),
            pltpu.VMEM((blocks, 16, f_block), F32),
            pltpu.VMEM((blocks, 2, 8, d_block), F32),
            pltpu.VMEM((blocks, 8, d_block), F32),
            pltpu.VMEM((n, 8, d_block), BF16),
            pltpu.VMEM((n, 8, d_block), BF16),
            pltpu.VMEM((n, 8, d_block), BF16),
            pltpu.VMEM((n, 8, d_block), BF16),
            dma((7,)),
            dma((n_sends,)),
            dma((n,)), dma((n,)), dma((n,)), dma((n,)),
            dma((2,)), dma((6,)),
            dma((n,)), dma((n,)), dma((n,)), dma((n,)),
            dma((4,)), dma((n,)),
        ],
        compiler_params=pltpu.CompilerParams(
            collective_id=0, has_side_effects=True, vmem_limit_bytes=40 * 1024 * 1024
        ),
    )(*(
        pltpu.with_memory_space_constraint(a, pltpu.HBM)
        for a in (upstream, tokens, gate_pre, up_pre, w_gate, w_up, w_down)
    ))

    scale = float(total) ** -0.5
    input_grad, gate_grad, up_grad, down_grad = pl.pallas_call(
        functools.partial(weight_grads, scale),
        name="weight_grads",
        grid=(2,),
        in_specs=[
            pl.BlockSpec((8, d_block), lambda i: (0, 0)),
            pl.BlockSpec((total, f_block), lambda i: (0, 0)),
            pl.BlockSpec((total, f_block), lambda i: (0, 0)),
            pl.BlockSpec((total, f_block // 2), lambda i: (0, i)),
            pl.BlockSpec((total, d_block // 2), lambda i: (0, i)),
            pl.BlockSpec((total, d_block), lambda i: (0, 0)),
        ],
        out_specs=[
            pl.BlockSpec((8, d_block), lambda i: (0, 0)),
            pl.BlockSpec((d_block // 2, f_block), lambda i: (i, 0)),
            pl.BlockSpec((d_block // 2, f_block), lambda i: (i, 0)),
            pl.BlockSpec((f_block // 2, d_block), lambda i: (i, 0)),
        ],
        out_shape=(
            jax.ShapeDtypeStruct((8, d_block), BF16),
            jax.ShapeDtypeStruct((d_block, f_block), BF16),
            jax.ShapeDtypeStruct((d_block, f_block), BF16),
            jax.ShapeDtypeStruct((f_block, d_block), BF16),
        ),
        compiler_params=pltpu.CompilerParams(vmem_limit_bytes=24 * 1024 * 1024),
    )(ig, gd, ud, hid, tok, ups)
    return (input_grad, gate_grad, up_grad, down_grad)


def solution(mesh):
    placed = (
        P("col", "row"),
        P("col", "row"),
        P("row", "col"),
        P("row", "col"),
        P("row", "col"),
        P("row", "col"),
        P("col", "row"),
    )
    return jax.shard_map(
        functools.partial(on_device, mesh.shape["row"] // 2),
        mesh=mesh,
        in_specs=placed,
        out_specs=(P("col", "row"), P("row", "col"), P("row", "col"), P("col", "row")),
        check_vma=False,
    )
```

```python
import functools

import jax
import jax.numpy as jnp
from jax import lax
from jax.experimental import pallas as pl
from jax.experimental.pallas import tpu as pltpu
from jax.sharding import PartitionSpec as P

MESH = pl.DeviceIdType.MESH
F32 = jnp.float32
BF16 = jnp.bfloat16
LAST = (((1,), (1,)), ((), ()))
FIRST = (((0,), (0,)), ((), ()))


def far_first(n):
    return sorted(range(1, n), key=lambda d: (-min(d, n - d), d))


def near_first(n):
    return sorted(range(1, n), key=lambda d: (min(d, n - d), d))


def exchange(
    n,
    ups, tok, gate, upre, w_gate, w_up, w_down,
    ig_out, gd_out, ud_out, hid_out, tok_out, ups_out,
    wg, wu, wd, ups_buf, tok_buf, gu_buf, part_buf, x_send, x_recv, z_send, z_recv,
    hg_buf, act, slope_up, ig_part, core_recv, y_send, y_recv,
    local_sem, send_sem, tok_sem, gu_sem, pair_sem,
    xr_sem, zr_sem, hz_sem, hx_sem, ig_y_sem, late_sem, ups_sem,
):
    row, col = lax.axis_index("row"), lax.axis_index("col")
    xh, z = row // n, lax.rem(row, n)
    y, q = col // 4, lax.rem(col, 4)
    xl, co = q // 2, lax.rem(q, 2)
    other = 1 - xh

    def z_peer(d):
        return (xh * n + lax.rem(z + d, n), col)

    def y_peer(d):
        return (row, lax.rem(y + d, n) * 4 + q)

    def yx_peer(d, e):
        return (row, lax.rem(y + d, n) * 4 + lax.rem(xl + e, 2) * 2 + co)

    offsets = [(d, e) for d in range(n) for e in range(2) if d or e]
    offsets.sort(key=lambda t: -min(t[0], n - t[0]) - t[1])
    xh_peer = (other * n + z, col)
    xl_peer = (row, y * 4 + (1 - xl) * 2 + co)
    co_peer = (row, y * 4 + xl * 2 + (1 - co))

    sends = []

    def send(src, dst, sem, device):
        copy = pltpu.make_async_remote_copy(
            src_ref=src, dst_ref=dst, send_sem=send_sem.at[len(sends)], recv_sem=sem,
            device_id=device, device_id_type=MESH,
        )
        copy.start()
        sends.append(copy)
        return copy

    def share(block, sem, device):
        return send(block, block, sem, device)

    locals_ = []

    def local(src, dst):
        copy = pltpu.make_async_copy(src, dst, local_sem.at[len(locals_)])
        copy.start()
        locals_.append(copy)
        return copy

    def wait_all(copies):
        for copy in copies:
            copy.wait_recv()

    barrier = pltpu.get_barrier_semaphore()
    peers = [yx_peer(d, e) for d, e in offsets] + [z_peer(d) for d in far_first(n)]
    peers += [xh_peer, co_peer]
    for device in peers:
        pl.semaphore_signal(barrier, inc=1, device_id=device, device_id_type=MESH)
    first_copies = [
        local(ups, ups_buf.at[co, y, xl]),
        local(gate, gu_buf.at[row, 0]),
        local(upre, gu_buf.at[row, 1]),
        local(tok, tok_buf.at[co, y, xl]),
    ]
    for copy in first_copies:
        copy.wait()
    pl.semaphore_wait(barrier, len(peers))

    ups_y = [share(ups_buf.at[co, y, xl], ups_sem.at[d, e], yx_peer(d, e)) for d, e in offsets]
    own_wd = local(w_down, wd)
    gu_z = [share(gu_buf.at[row], gu_sem.at[d], z_peer(d)) for d in near_first(n)]
    tok_xl = share(tok_buf.at[co, y, xl], pair_sem.at[1], xl_peer)
    wait_all(ups_y[::-1])
    ups_co = share(ups_buf.at[co], pair_sem.at[2], co_peer)
    tok_xl.wait_recv()
    tok_y = [share(tok_buf.at[co, y], tok_sem.at[d], y_peer(d)) for d in far_first(n)]

    half = 16 * n
    near_rows = pl.ds(pl.multiple_of(xh * half, half), half)
    far_rows = pl.ds(pl.multiple_of(other * half, half), half)
    near_blocks, far_blocks = pl.ds(xh * n, n), pl.ds(other * n, n)

    def hidden_part(core):
        rows = ups_buf[core].astype(F32).reshape(half, ups.shape[-1]).astype(BF16)
        part = lax.dot_general(rows, wd[...], LAST, preferred_element_type=F32)
        part_buf[core] = part.reshape(2 * n, 8, part.shape[-1])

    own_wd.wait()
    hidden_part(co)

    x_send[co] = part_buf[co, far_blocks].astype(BF16)
    first_x = send(x_send.at[co], x_recv.at[co], xr_sem.at[n], xh_peer)
    ups_co.wait_recv()
    hidden_part(1 - co)
    x_order = far_first(n) + [0]
    parts_x = []
    for d in x_order:
        k = lax.rem(z + d, n)
        x_send[1 - co, k] = part_buf[1 - co, other * n + k].astype(BF16)
        parts_x.append(send(x_send.at[1 - co, k], x_recv.at[1 - co, k], xr_sem.at[d], xh_peer))
    own_wg = local(w_gate, wg)
    own_wu = local(w_up, wu)

    def order_tokens(buf, out):
        @pl.loop(0, n)
        def _(k):
            rows = jnp.stack([buf[0, k].astype(F32), buf[1, k].astype(F32)], axis=1)
            rows = rows.reshape(32, buf.shape[-1])
            out[pl.ds(pl.multiple_of(k * 32, 32), 32), :] = rows.astype(BF16)

    order_tokens(ups_buf, ups_out)

    parts_z = []
    first_x.wait_recv()
    for d, part_x in zip(x_order, parts_x):
        k = lax.rem(z + d, n)
        part_x.wait_recv()
        total = part_buf[:, xh * n + k] + x_recv[:, k].astype(F32)
        if d:
            z_send[k] = total.astype(BF16)
            parts_z.append(send(z_send.at[k], z_recv.at[d], zr_sem.at[d], z_peer(d)))
    part_buf[:, row] = total

    wait_all(gu_z)
    gu_x = share(gu_buf.at[near_blocks], gu_sem.at[0], xh_peer)
    wait_all(tok_y)
    tok_co = share(tok_buf.at[co], pair_sem.at[3], co_peer)

    def activations(first):
        @pl.loop(0, n)
        def _(j):
            k = first + j
            g = gu_buf[k, 0].astype(F32)
            u = gu_buf[k, 1].astype(F32)
            s = jax.nn.sigmoid(g)
            activated = g * s
            act[k] = activated
            slope_up[k] = u * (s * (1.0 + g * (1.0 - s)))
            hid_out[pl.ds(pl.multiple_of(k * 16, 16), 16), :] = (activated * u).astype(BF16)

    activations(xh * n)

    total = part_buf[:, row]
    for d, part_z in zip(far_first(n)[::-1], parts_z[::-1]):
        part_z.wait_recv()
        total = total + z_recv[d].astype(F32)
    hg_buf[row] = total.reshape(16, total.shape[-1]).astype(BF16)
    hg_z = [share(hg_buf.at[row], hz_sem.at[d], z_peer(d)) for d in near_first(n)]
    hg_x = [share(hg_buf.at[row], hx_sem.at[0], xh_peer)]

    tok_co.wait_recv()
    order_tokens(tok_buf, tok_out)
    own_wg.wait()
    own_wu.wait()

    for d, copy in zip(near_first(n), hg_z):
        copy.wait_recv()
        block = hg_buf.at[xh * n + lax.rem(z - d + n, n)]
        hg_x.append(share(block, hx_sem.at[d], xh_peer))

    def deltas(first):
        @pl.loop(0, n)
        def _(j):
            k = first + j
            grad = hg_buf[k].astype(F32)
            rows = pl.ds(pl.multiple_of(k * 16, 16), 16)
            gd_out[rows, :] = (grad * slope_up[k]).astype(BF16)
            ud_out[rows, :] = (grad * act[k]).astype(BF16)

    def input_part(rows, blocks, sem):
        part = lax.dot_general(gd_out[rows, :], wg[...], LAST, preferred_element_type=F32)
        part = part + lax.dot_general(ud_out[rows, :], wu[...], LAST, preferred_element_type=F32)
        ig_part[blocks] = part.reshape(n, 2, 8, part.shape[-1])
        return send(ig_part.at[blocks, 1 - co], core_recv.at[blocks], sem, co_peer)

    def pair_sum(k):
        return ig_part[k, co] + core_recv[k]

    late = []

    def to_y(first):
        for j in range(n):
            k = first + j
            y_send[k] = pair_sum(k).astype(BF16)
            copy = pltpu.make_async_remote_copy(
                src_ref=y_send.at[k], dst_ref=y_recv.at[2 * y + xl],
                send_sem=late_sem.at[len(late)], recv_sem=ig_y_sem.at[2 * y + xl],
                device_id=(row, k * 2 + co), device_id_type=MESH,
            )
            late.append((k, copy))

            @pl.when(k != 2 * y + xl)
            def _():
                copy.start()

    deltas(xh * n)
    near_co = input_part(near_rows, near_blocks, pair_sem.at[4])
    gu_x.wait_recv()
    activations(other * n)
    wait_all(hg_x)
    deltas(other * n)
    far_co = input_part(far_rows, far_blocks, pair_sem.at[5])
    near_co.wait_recv()
    to_y(xh * n)
    far_co.wait_recv()
    to_y(other * n)

    total = pair_sum(2 * y + xl)
    for d, e in offsets[::-1]:
        k = 2 * lax.rem(y - d + n, n) + lax.rem(xl + e, 2)
        pltpu.make_async_remote_copy(
            src_ref=y_send.at[k], dst_ref=y_recv.at[k], send_sem=send_sem.at[0],
            recv_sem=ig_y_sem.at[k], device_id=co_peer, device_id_type=MESH,
        ).wait_recv()
        total = total + y_recv[k].astype(F32)
    ig_out[...] = total.astype(BF16)

    for copy in sends:
        copy.wait_send()
    for k, copy in late:

        @pl.when(k != 2 * y + xl)
        def _():
            copy.wait_send()


def weight_grads(
    scale, ig, gd, ud, hid, tok, ups, input_grad, gate_grad, up_grad, down_grad,
    gate_buf, up_buf, down_buf, sem,
):
    copies = []

    def chunk(a, first, rows, b, buf, out):
        left = a[:, first : first + rows]
        part = lax.dot_general(left, b[...], FIRST, preferred_element_type=F32) * scale
        buf[pl.ds(first, rows), :] = part.astype(BF16)
        copies.append(
            pltpu.make_async_copy(
                buf.at[pl.ds(first, rows)], out.at[pl.ds(first, rows)], sem.at[len(copies)]
            )
        )
        copies[-1].start()

    copies.append(pltpu.make_async_copy(ig, input_grad, sem.at[0]))
    copies[-1].start()
    for a, b, buf, out in (
        (tok, gd, gate_buf, gate_grad), (tok, ud, up_buf, up_grad), (hid, ups, down_buf, down_grad)
    ):
        for first in range(0, a.shape[1], 256):
            chunk(a, first, 256, b, buf, out)
    for copy in copies:
        copy.wait()


def on_device(n, tokens, upstream, gate_pre, up_pre, w_gate, w_up, w_down):
    d_block, f_block = w_gate.shape
    total = 32 * n
    blocks = 2 * n
    dma = pltpu.SemaphoreType.DMA
    hbm_spec = pl.BlockSpec(memory_space=pltpu.HBM)
    vmem_spec = pl.BlockSpec(memory_space=pltpu.VMEM)
    n_sends = 8 * n + 2
    ig, gd, ud, hid, tok, ups = pl.pallas_call(
        functools.partial(exchange, n),
        name="exchange",
        out_shape=(
            jax.ShapeDtypeStruct((8, d_block), BF16),
            jax.ShapeDtypeStruct((total, f_block), BF16),
            jax.ShapeDtypeStruct((total, f_block), BF16),
            jax.ShapeDtypeStruct((total, f_block), BF16),
            jax.ShapeDtypeStruct((total, d_block), BF16),
            jax.ShapeDtypeStruct((total, d_block), BF16),
        ),
        in_specs=[hbm_spec] * 7,
        out_specs=[vmem_spec] * 6,
        scratch_shapes=[
            pltpu.VMEM((d_block, f_block), BF16),
            pltpu.VMEM((d_block, f_block), BF16),
            pltpu.VMEM((f_block, d_block), BF16),
            pltpu.VMEM((2, n, 2, 8, d_block), BF16),
            pltpu.VMEM((2, n, 2, 8, d_block), BF16),
            pltpu.VMEM((blocks, 2, 16, f_block), BF16),
            pltpu.VMEM((2, blocks, 8, f_block), F32),
            pltpu.VMEM((2, n, 8, f_block), BF16),
            pltpu.VMEM((2, n, 8, f_block), BF16),
            pltpu.VMEM((n, 2, 8, f_block), BF16),
            pltpu.VMEM((n, 2, 8, f_block), BF16),
            pltpu.VMEM((blocks, 16, f_block), BF16),
            pltpu.VMEM((blocks, 16, f_block), F32),
            pltpu.VMEM((blocks, 16, f_block), F32),
            pltpu.VMEM((blocks, 2, 8, d_block), F32),
            pltpu.VMEM((blocks, 8, d_block), F32),
            pltpu.VMEM((blocks, 8, d_block), BF16),
            pltpu.VMEM((blocks, 8, d_block), BF16),
            dma((7,)),
            dma((n_sends,)),
            dma((n,)), dma((n,)), dma((7,)),
            dma((n + 1,)), dma((n,)), dma((n,)), dma((n,)), dma((2 * n,)), dma((2 * n,)), dma((n, 2)),
        ],
        compiler_params=pltpu.CompilerParams(
            collective_id=0, has_side_effects=True, vmem_limit_bytes=40 * 1024 * 1024
        ),
    )(*(
        pltpu.with_memory_space_constraint(a, pltpu.HBM)
        for a in (upstream, tokens, gate_pre, up_pre, w_gate, w_up, w_down)
    ))

    scale = float(total) ** -0.5
    input_grad, gate_grad, up_grad, down_grad = pl.pallas_call(
        functools.partial(weight_grads, scale),
        name="weight_grads",
        in_specs=[vmem_spec] * 6,
        out_specs=[pl.BlockSpec(memory_space=pl.ANY)] * 4,
        out_shape=(
            jax.ShapeDtypeStruct((8, d_block), BF16),
            jax.ShapeDtypeStruct((d_block, f_block), BF16),
            jax.ShapeDtypeStruct((d_block, f_block), BF16),
            jax.ShapeDtypeStruct((f_block, d_block), BF16),
        ),
        scratch_shapes=[
            pltpu.VMEM((d_block, f_block), BF16),
            pltpu.VMEM((d_block, f_block), BF16),
            pltpu.VMEM((f_block, d_block), BF16),
            dma((1 + (2 * d_block + f_block) // 256,)),
        ],
        compiler_params=pltpu.CompilerParams(vmem_limit_bytes=24 * 1024 * 1024),
    )(ig, gd, ud, hid, tok, ups)
    return (input_grad, gate_grad, up_grad, down_grad)


def solution(mesh):
    placed = (
        P("col", "row"),
        P("col", "row"),
        P("row", "col"),
        P("row", "col"),
        P("row", "col"),
        P("row", "col"),
        P("col", "row"),
    )
    return jax.shard_map(
        functools.partial(on_device, mesh.shape["row"] // 2),
        mesh=mesh,
        in_specs=placed,
        out_specs=(P("col", "row"), P("row", "col"), P("row", "col"), P("col", "row")),
        check_vma=False,
    )
```

```python
import functools

import jax
import jax.numpy as jnp
from jax import lax
from jax.experimental import pallas as pl
from jax.experimental.pallas import tpu as pltpu
from jax.sharding import PartitionSpec as P

MESH = pl.DeviceIdType.MESH
F32 = jnp.float32
BF16 = jnp.bfloat16
LAST = (((1,), (1,)), ((), ()))
FIRST = (((0,), (0,)), ((), ()))


def far_first(n):
    return sorted(range(1, n), key=lambda d: (-min(d, n - d), d))


def near_first(n):
    return sorted(range(1, n), key=lambda d: (min(d, n - d), d))


def exchange(
    n, scale,
    ups, tok, gate, upre, w_gate, w_up, w_down,
    ig_out, gate_out, up_out, down_out,
    gd_out, ud_out, hid_out, tok_out, ups_out,
    wg, wu, wd, ups_buf, tok_buf, gu_buf, part_buf, x_send, x_recv, z_send, z_recv,
    hg_buf, act, slope_up, ig_part, core_recv, y_send, y_recv,
    local_sem, send_sem, tok_sem, gu_sem, pair_sem,
    xr_sem, zr_sem, hz_sem, hx_sem, ig_y_sem, late_sem, ups_sem,
):
    row, col = lax.axis_index("row"), lax.axis_index("col")
    xh, z = row // n, lax.rem(row, n)
    y, q = col // 4, lax.rem(col, 4)
    xl, co = q // 2, lax.rem(q, 2)
    other = 1 - xh

    def z_peer(d):
        return (xh * n + lax.rem(z + d, n), col)

    def y_peer(d):
        return (row, lax.rem(y + d, n) * 4 + q)

    def yx_peer(d, e):
        return (row, lax.rem(y + d, n) * 4 + lax.rem(xl + e, 2) * 2 + co)

    offsets = [(d, e) for d in range(n) for e in range(2) if d or e]
    offsets.sort(key=lambda t: -min(t[0], n - t[0]) - t[1])
    xh_peer = (other * n + z, col)
    xl_peer = (row, y * 4 + (1 - xl) * 2 + co)
    co_peer = (row, y * 4 + xl * 2 + (1 - co))

    sends = []

    def send(src, dst, sem, device):
        copy = pltpu.make_async_remote_copy(
            src_ref=src, dst_ref=dst, send_sem=send_sem.at[len(sends)], recv_sem=sem,
            device_id=device, device_id_type=MESH,
        )
        copy.start()
        sends.append(copy)
        return copy

    def share(block, sem, device):
        return send(block, block, sem, device)

    locals_ = []

    def local(src, dst):
        copy = pltpu.make_async_copy(src, dst, local_sem.at[len(locals_)])
        copy.start()
        locals_.append(copy)
        return copy

    def wait_all(copies):
        for copy in copies:
            copy.wait_recv()

    barrier = pltpu.get_barrier_semaphore()
    peers = [yx_peer(d, e) for d, e in offsets] + [z_peer(d) for d in far_first(n)]
    peers += [xh_peer, co_peer]
    first_copies = [local(ups, ups_buf.at[co, y, xl])]
    for device in peers:
        pl.semaphore_signal(barrier, inc=1, device_id=device, device_id_type=MESH)
    first_copies += [
        local(gate, gu_buf.at[row, 0]),
        local(upre, gu_buf.at[row, 1]),
        local(tok, tok_buf.at[co, y, xl]),
    ]
    first_copies[0].wait()
    pl.semaphore_wait(barrier, len(peers))

    ups_y = [share(ups_buf.at[co, y, xl], ups_sem.at[d, e], yx_peer(d, e)) for d, e in offsets]
    own_wd = local(w_down, wd)
    for copy in first_copies[1:]:
        copy.wait()
    gu_z = [share(gu_buf.at[row], gu_sem.at[d], z_peer(d)) for d in near_first(n)]
    tok_xl = share(tok_buf.at[co, y, xl], pair_sem.at[1], xl_peer)
    wait_all(ups_y[::-1])
    ups_co = share(ups_buf.at[co], pair_sem.at[2], co_peer)
    tok_xl.wait_recv()
    tok_y = [share(tok_buf.at[co, y], tok_sem.at[d], y_peer(d)) for d in far_first(n)]

    half = 16 * n
    near_rows = pl.ds(pl.multiple_of(xh * half, half), half)
    far_rows = pl.ds(pl.multiple_of(other * half, half), half)
    near_blocks, far_blocks = pl.ds(xh * n, n), pl.ds(other * n, n)

    def hidden_part(core):
        rows = ups_buf[core].astype(F32).reshape(half, ups.shape[-1]).astype(BF16)
        part = lax.dot_general(rows, wd[...], LAST, preferred_element_type=F32)
        part_buf[core] = part.reshape(2 * n, 8, part.shape[-1])

    own_wd.wait()
    hidden_part(co)

    x_send[co] = part_buf[co, far_blocks].astype(BF16)
    first_x = send(x_send.at[co], x_recv.at[co], xr_sem.at[n], xh_peer)
    ups_co.wait_recv()
    hidden_part(1 - co)
    x_order = far_first(n) + [0]
    parts_x = []
    for d in x_order:
        k = lax.rem(z + d, n)
        x_send[1 - co, k] = part_buf[1 - co, other * n + k].astype(BF16)
        parts_x.append(send(x_send.at[1 - co, k], x_recv.at[1 - co, k], xr_sem.at[d], xh_peer))
    own_wg = local(w_gate, wg)
    own_wu = local(w_up, wu)

    def order_tokens(buf, out):
        @pl.loop(0, n)
        def _(k):
            rows = jnp.stack([buf[0, k].astype(F32), buf[1, k].astype(F32)], axis=1)
            rows = rows.reshape(32, buf.shape[-1])
            out[pl.ds(pl.multiple_of(k * 32, 32), 32), :] = rows.astype(BF16)

    order_tokens(ups_buf, ups_out)

    parts_z = []
    first_x.wait_recv()
    for d, part_x in zip(x_order, parts_x):
        k = lax.rem(z + d, n)
        part_x.wait_recv()
        total = part_buf[:, xh * n + k] + x_recv[:, k].astype(F32)
        if d:
            z_send[k] = total.astype(BF16)
            parts_z.append(send(z_send.at[k], z_recv.at[d], zr_sem.at[d], z_peer(d)))
    part_buf[:, row] = total

    wait_all(gu_z)
    gu_x = share(gu_buf.at[near_blocks], gu_sem.at[0], xh_peer)
    wait_all(tok_y)
    tok_co = share(tok_buf.at[co], pair_sem.at[3], co_peer)

    def activations(first):
        @pl.loop(0, n)
        def _(j):
            k = first + j
            g = gu_buf[k, 0].astype(F32)
            u = gu_buf[k, 1].astype(F32)
            s = jax.nn.sigmoid(g)
            activated = g * s
            act[k] = activated
            slope_up[k] = u * (s * (1.0 + g * (1.0 - s)))
            hid_out[pl.ds(pl.multiple_of(k * 16, 16), 16), :] = (activated * u).astype(BF16)

    activations(xh * n)

    total = part_buf[:, row]
    for d, part_z in zip(far_first(n)[::-1], parts_z[::-1]):
        part_z.wait_recv()
        total = total + z_recv[d].astype(F32)
    hg_buf[row] = total.reshape(16, total.shape[-1]).astype(BF16)
    hg_x = [share(hg_buf.at[row], hx_sem.at[0], xh_peer)]
    hg_z = [share(hg_buf.at[row], hz_sem.at[d], z_peer(d)) for d in near_first(n)]

    tok_co.wait_recv()
    order_tokens(tok_buf, tok_out)
    own_wg.wait()
    own_wu.wait()

    for d, copy in zip(near_first(n), hg_z):
        copy.wait_recv()
        block = hg_buf.at[xh * n + lax.rem(z - d + n, n)]
        hg_x.append(share(block, hx_sem.at[d], xh_peer))

    def deltas(first):
        @pl.loop(0, n)
        def _(j):
            k = first + j
            grad = hg_buf[k].astype(F32)
            rows = pl.ds(pl.multiple_of(k * 16, 16), 16)
            gd_out[rows, :] = (grad * slope_up[k]).astype(BF16)
            ud_out[rows, :] = (grad * act[k]).astype(BF16)

    def input_part(rows, blocks, sem):
        part = lax.dot_general(gd_out[rows, :], wg[...], LAST, preferred_element_type=F32)
        part = part + lax.dot_general(ud_out[rows, :], wu[...], LAST, preferred_element_type=F32)
        ig_part[blocks] = part.reshape(n, 2, 8, part.shape[-1])
        return send(ig_part.at[blocks, 1 - co], core_recv.at[blocks], sem, co_peer)

    def pair_sum(k):
        return ig_part[k, co] + core_recv[k]

    late = []

    def to_y(first):
        for j in range(n):
            k = first + j
            y_send[k] = pair_sum(k).astype(BF16)
            copy = pltpu.make_async_remote_copy(
                src_ref=y_send.at[k], dst_ref=y_recv.at[2 * y + xl],
                send_sem=late_sem.at[len(late)], recv_sem=ig_y_sem.at[2 * y + xl],
                device_id=(row, k * 2 + co), device_id_type=MESH,
            )
            late.append((k, copy))

            @pl.when(k != 2 * y + xl)
            def _():
                copy.start()

    deltas(xh * n)
    near_co = input_part(near_rows, near_blocks, pair_sem.at[4])
    gu_x.wait_recv()
    activations(other * n)
    wait_all(hg_x)
    deltas(other * n)
    far_co = input_part(far_rows, far_blocks, pair_sem.at[5])
    near_co.wait_recv()
    to_y(xh * n)
    far_co.wait_recv()
    to_y(other * n)

    @pl.loop(0, tok_out.shape[1] // 256)
    def _(i):
        columns = pl.ds(pl.multiple_of(i * 256, 256), 256)
        for delta, out in ((gd_out, gate_out), (ud_out, up_out)):
            part = lax.dot_general(tok_out[:, columns], delta[...], FIRST, preferred_element_type=F32)
            out[columns, :] = (part * scale).astype(BF16)

    @pl.loop(0, hid_out.shape[1] // 256)
    def _(i):
        columns = pl.ds(pl.multiple_of(i * 256, 256), 256)
        part = lax.dot_general(hid_out[:, columns], ups_out[...], FIRST, preferred_element_type=F32)
        down_out[columns, :] = (part * scale).astype(BF16)

    total = pair_sum(2 * y + xl)
    for d, e in offsets[::-1]:
        k = 2 * lax.rem(y - d + n, n) + lax.rem(xl + e, 2)
        pltpu.make_async_remote_copy(
            src_ref=y_send.at[k], dst_ref=y_recv.at[k], send_sem=send_sem.at[0],
            recv_sem=ig_y_sem.at[k], device_id=co_peer, device_id_type=MESH,
        ).wait_recv()
        total = total + y_recv[k].astype(F32)
    ig_out[...] = total.astype(BF16)

    for copy in sends:
        copy.wait_send()
    for k, copy in late:

        @pl.when(k != 2 * y + xl)
        def _():
            copy.wait_send()


def write_out(*refs):
    *pairs, sem = refs
    copies = []
    for src, dst in zip(pairs[:4], pairs[4:]):
        parts = 1 if src.shape[0] < 256 else 2
        rows = src.shape[0] // parts
        for k in range(parts):
            copies.append(
                pltpu.make_async_copy(
                    src.at[pl.ds(k * rows, rows)], dst.at[pl.ds(k * rows, rows)], sem.at[len(copies)]
                )
            )
            copies[-1].start()
    for copy in copies:
        copy.wait()


def on_device(n, tokens, upstream, gate_pre, up_pre, w_gate, w_up, w_down):
    d_block, f_block = w_gate.shape
    total = 32 * n
    blocks = 2 * n
    dma = pltpu.SemaphoreType.DMA
    hbm_spec = pl.BlockSpec(memory_space=pltpu.HBM)
    vmem_spec = pl.BlockSpec(memory_space=pltpu.VMEM)
    n_sends = 8 * n + 2
    grad_shapes = (
        jax.ShapeDtypeStruct((8, d_block), BF16),
        jax.ShapeDtypeStruct((d_block, f_block), BF16),
        jax.ShapeDtypeStruct((d_block, f_block), BF16),
        jax.ShapeDtypeStruct((f_block, d_block), BF16),
    )
    grads = pl.pallas_call(
        functools.partial(exchange, n, float(total) ** -0.5),
        name="exchange",
        out_shape=grad_shapes,
        in_specs=[hbm_spec] * 7,
        out_specs=[vmem_spec] * 4,
        scratch_shapes=[
            pltpu.VMEM((total, f_block), BF16),
            pltpu.VMEM((total, f_block), BF16),
            pltpu.VMEM((total, f_block), BF16),
            pltpu.VMEM((total, d_block), BF16),
            pltpu.VMEM((total, d_block), BF16),
            pltpu.VMEM((d_block, f_block), BF16),
            pltpu.VMEM((d_block, f_block), BF16),
            pltpu.VMEM((f_block, d_block), BF16),
            pltpu.VMEM((2, n, 2, 8, d_block), BF16),
            pltpu.VMEM((2, n, 2, 8, d_block), BF16),
            pltpu.VMEM((blocks, 2, 16, f_block), BF16),
            pltpu.VMEM((2, blocks, 8, f_block), F32),
            pltpu.VMEM((2, n, 8, f_block), BF16),
            pltpu.VMEM((2, n, 8, f_block), BF16),
            pltpu.VMEM((n, 2, 8, f_block), BF16),
            pltpu.VMEM((n, 2, 8, f_block), BF16),
            pltpu.VMEM((blocks, 16, f_block), BF16),
            pltpu.VMEM((blocks, 16, f_block), F32),
            pltpu.VMEM((blocks, 16, f_block), F32),
            pltpu.VMEM((blocks, 2, 8, d_block), F32),
            pltpu.VMEM((blocks, 8, d_block), F32),
            pltpu.VMEM((blocks, 8, d_block), BF16),
            pltpu.VMEM((blocks, 8, d_block), BF16),
            dma((7,)),
            dma((n_sends,)),
            dma((n,)), dma((n,)), dma((7,)),
            dma((n + 1,)), dma((n,)), dma((n,)), dma((n,)), dma((2 * n,)), dma((2 * n,)), dma((n, 2)),
        ],
        compiler_params=pltpu.CompilerParams(
            collective_id=0, has_side_effects=True, vmem_limit_bytes=40 * 1024 * 1024
        ),
    )(*(
        pltpu.with_memory_space_constraint(a, pltpu.HBM)
        for a in (upstream, tokens, gate_pre, up_pre, w_gate, w_up, w_down)
    ))

    return pl.pallas_call(
        write_out,
        name="write_out",
        in_specs=[vmem_spec] * 4,
        out_specs=[pl.BlockSpec(memory_space=pl.ANY)] * 4,
        out_shape=grad_shapes,
        scratch_shapes=[dma((7,))],
        compiler_params=pltpu.CompilerParams(vmem_limit_bytes=16 * 1024 * 1024),
    )(*grads)


def solution(mesh):
    placed = (
        P("col", "row"),
        P("col", "row"),
        P("row", "col"),
        P("row", "col"),
        P("row", "col"),
        P("row", "col"),
        P("col", "row"),
    )
    return jax.shard_map(
        functools.partial(on_device, mesh.shape["row"] // 2),
        mesh=mesh,
        in_specs=placed,
        out_specs=(P("col", "row"), P("row", "col"), P("row", "col"), P("col", "row")),
        check_vma=False,
    )
```

```python
import functools

import jax
import jax.numpy as jnp
from jax import lax
from jax.experimental import pallas as pl
from jax.experimental.pallas import tpu as pltpu
from jax.sharding import PartitionSpec as P

MESH = pl.DeviceIdType.MESH
F32 = jnp.float32
BF16 = jnp.bfloat16
LAST = (((1,), (1,)), ((), ()))
FIRST = (((0,), (0,)), ((), ()))


def far_first(n):
    return sorted(range(1, n), key=lambda d: (-min(d, n - d), d))


def near_first(n):
    return sorted(range(1, n), key=lambda d: (min(d, n - d), d))


def exchange(
    n, scale,
    ups, tok, gate, upre, w_gate, w_up, w_down,
    ig_out, gate_out, up_out, down_out,
    gd_out, ud_out, hid_out, tok_out, ups_out,
    wg, wu, wd, ups_buf, tok_buf, gu_buf, part_buf, x_send, x_recv, z_send, z_recv,
    hg_buf, act, slope_up, ig_part, core_recv, y_send, y_recv,
    local_sem, send_sem, tok_sem, gu_sem, pair_sem,
    xr_sem, zr_sem, hz_sem, hx_sem, ig_y_sem, late_sem, ups_sem,
):
    row, col = lax.axis_index("row"), lax.axis_index("col")
    xh, z = row // n, lax.rem(row, n)
    y, q = col // 4, lax.rem(col, 4)
    xl, co = q // 2, lax.rem(q, 2)
    other = 1 - xh

    def z_peer(d):
        return (xh * n + lax.rem(z + d, n), col)

    def y_peer(d):
        return (row, lax.rem(y + d, n) * 4 + q)

    def yx_peer(d, e):
        return (row, lax.rem(y + d, n) * 4 + lax.rem(xl + e, 2) * 2 + co)

    offsets = [(d, e) for d in range(n) for e in range(2) if d or e]
    offsets.sort(key=lambda t: -min(t[0], n - t[0]) - t[1])
    xh_peer = (other * n + z, col)
    xl_peer = (row, y * 4 + (1 - xl) * 2 + co)
    co_peer = (row, y * 4 + xl * 2 + (1 - co))

    sends = []

    def send(src, dst, sem, device):
        copy = pltpu.make_async_remote_copy(
            src_ref=src, dst_ref=dst, send_sem=send_sem.at[len(sends)], recv_sem=sem,
            device_id=device, device_id_type=MESH,
        )
        copy.start()
        sends.append(copy)
        return copy

    def share(block, sem, device):
        return send(block, block, sem, device)

    locals_ = []

    def local(src, dst):
        copy = pltpu.make_async_copy(src, dst, local_sem.at[len(locals_)])
        copy.start()
        locals_.append(copy)
        return copy

    def wait_all(copies):
        for copy in copies:
            copy.wait_recv()

    barrier = pltpu.get_barrier_semaphore()
    peers = [yx_peer(d, e) for d, e in offsets] + [z_peer(d) for d in far_first(n)]
    peers += [xh_peer, co_peer]
    first_copies = [local(ups, ups_buf.at[co, y, xl])]
    for device in peers:
        pl.semaphore_signal(barrier, inc=1, device_id=device, device_id_type=MESH)
    first_copies += [
        local(gate, gu_buf.at[row, 0]),
        local(upre, gu_buf.at[row, 1]),
        local(tok, tok_buf.at[co, y, xl]),
    ]
    first_copies[0].wait()
    pl.semaphore_wait(barrier, len(peers))

    ups_y = [share(ups_buf.at[co, y, xl], ups_sem.at[d, e], yx_peer(d, e)) for d, e in offsets]
    own_wd = local(w_down, wd)
    for copy in first_copies[1:]:
        copy.wait()
    gu_z = [share(gu_buf.at[row], gu_sem.at[d], z_peer(d)) for d in near_first(n)]
    tok_xl = share(tok_buf.at[co, y, xl], pair_sem.at[1], xl_peer)
    wait_all(ups_y[::-1])
    ups_co = share(ups_buf.at[co], pair_sem.at[2], co_peer)
    tok_xl.wait_recv()
    tok_y = [share(tok_buf.at[co, y], tok_sem.at[d], y_peer(d)) for d in far_first(n)]

    half = 16 * n
    near_rows = pl.ds(pl.multiple_of(xh * half, half), half)
    far_rows = pl.ds(pl.multiple_of(other * half, half), half)
    near_blocks, far_blocks = pl.ds(xh * n, n), pl.ds(other * n, n)

    def hidden_part(core):
        rows = ups_buf[core].astype(F32).reshape(half, ups.shape[-1]).astype(BF16)
        part = lax.dot_general(rows, wd[...], LAST, preferred_element_type=F32)
        part_buf[core] = part.reshape(2 * n, 8, part.shape[-1])

    own_wd.wait()
    hidden_part(co)

    x_send[co] = part_buf[co, far_blocks].astype(BF16)
    first_x = send(x_send.at[co], x_recv.at[co], xr_sem.at[n], xh_peer)
    ups_co.wait_recv()
    hidden_part(1 - co)
    x_order = far_first(n) + [0]
    parts_x = []
    for d in x_order:
        k = lax.rem(z + d, n)
        x_send[1 - co, k] = part_buf[1 - co, other * n + k].astype(BF16)
        parts_x.append(send(x_send.at[1 - co, k], x_recv.at[1 - co, k], xr_sem.at[d], xh_peer))
    own_wg = local(w_gate, wg)
    own_wu = local(w_up, wu)

    def order_tokens(buf, out):
        @pl.loop(0, n)
        def _(k):
            rows = jnp.stack([buf[0, k].astype(F32), buf[1, k].astype(F32)], axis=1)
            rows = rows.reshape(32, buf.shape[-1])
            out[pl.ds(pl.multiple_of(k * 32, 32), 32), :] = rows.astype(BF16)

    order_tokens(ups_buf, ups_out)

    parts_z = []

    def sum_pair(core, step, d):
        k = lax.rem(z + d, n)
        total = part_buf[core, xh * n + k] + x_recv[core, k].astype(F32)
        if d:
            z_send[k, core] = total.astype(BF16)
            parts_z.append(
                send(z_send.at[k, core], z_recv.at[d, core], zr_sem.at[step, d], z_peer(d))
            )
        else:
            part_buf[core, row] = total

    first_x.wait_recv()
    for d in x_order:
        sum_pair(co, 0, d)
    for d, part_x in zip(x_order, parts_x):
        part_x.wait_recv()
        sum_pair(1 - co, 1, d)

    wait_all(gu_z)
    gu_x = share(gu_buf.at[near_blocks], gu_sem.at[0], xh_peer)
    wait_all(tok_y)
    tok_co = share(tok_buf.at[co], pair_sem.at[3], co_peer)

    def activations(first):
        @pl.loop(0, n)
        def _(j):
            k = first + j
            g = gu_buf[k, 0].astype(F32)
            u = gu_buf[k, 1].astype(F32)
            s = jax.nn.sigmoid(g)
            activated = g * s
            act[k] = activated
            slope_up[k] = u * (s * (1.0 + g * (1.0 - s)))
            hid_out[pl.ds(pl.multiple_of(k * 16, 16), 16), :] = (activated * u).astype(BF16)

    activations(xh * n)

    total = part_buf[:, row]
    wait_all(parts_z[: n - 1])
    for d, part_z in zip(far_first(n)[::-1], parts_z[: n - 2 : -1]):
        part_z.wait_recv()
        total = total + z_recv[d].astype(F32)
    hg_buf[row] = total.reshape(16, total.shape[-1]).astype(BF16)
    hg_x = [share(hg_buf.at[row], hx_sem.at[0], xh_peer)]
    hg_z = [share(hg_buf.at[row], hz_sem.at[d], z_peer(d)) for d in near_first(n)]

    tok_co.wait_recv()
    order_tokens(tok_buf, tok_out)
    own_wg.wait()
    own_wu.wait()

    for d, copy in zip(near_first(n), hg_z):
        copy.wait_recv()
        block = hg_buf.at[xh * n + lax.rem(z - d + n, n)]
        hg_x.append(share(block, hx_sem.at[d], xh_peer))

    def deltas(first):
        @pl.loop(0, n)
        def _(j):
            k = first + j
            grad = hg_buf[k].astype(F32)
            rows = pl.ds(pl.multiple_of(k * 16, 16), 16)
            gd_out[rows, :] = (grad * slope_up[k]).astype(BF16)
            ud_out[rows, :] = (grad * act[k]).astype(BF16)

    def input_part(rows, blocks, sem):
        part = lax.dot_general(gd_out[rows, :], wg[...], LAST, preferred_element_type=F32)
        part = part + lax.dot_general(ud_out[rows, :], wu[...], LAST, preferred_element_type=F32)
        ig_part[blocks] = part.reshape(n, 2, 8, part.shape[-1])
        return send(ig_part.at[blocks, 1 - co], core_recv.at[blocks], sem, co_peer)

    def pair_sum(k):
        return ig_part[k, co] + core_recv[k]

    late = []

    def to_y(first):
        for j in range(n):
            k = first + j
            y_send[k] = pair_sum(k).astype(BF16)
            copy = pltpu.make_async_remote_copy(
                src_ref=y_send.at[k], dst_ref=y_recv.at[2 * y + xl],
                send_sem=late_sem.at[len(late)], recv_sem=ig_y_sem.at[2 * y + xl],
                device_id=(row, k * 2 + co), device_id_type=MESH,
            )
            late.append((k, copy))

            @pl.when(k != 2 * y + xl)
            def _():
                copy.start()

    deltas(xh * n)
    near_co = input_part(near_rows, near_blocks, pair_sem.at[4])
    gu_x.wait_recv()
    activations(other * n)
    wait_all(hg_x)
    deltas(other * n)
    far_co = input_part(far_rows, far_blocks, pair_sem.at[5])
    near_co.wait_recv()
    to_y(xh * n)
    far_co.wait_recv()
    to_y(other * n)

    @pl.loop(0, tok_out.shape[1] // 256)
    def _(i):
        columns = pl.ds(pl.multiple_of(i * 256, 256), 256)
        for delta, out in ((gd_out, gate_out), (ud_out, up_out)):
            part = lax.dot_general(tok_out[:, columns], delta[...], FIRST, preferred_element_type=F32)
            out[columns, :] = (part * scale).astype(BF16)

    @pl.loop(0, hid_out.shape[1] // 256)
    def _(i):
        columns = pl.ds(pl.multiple_of(i * 256, 256), 256)
        part = lax.dot_general(hid_out[:, columns], ups_out[...], FIRST, preferred_element_type=F32)
        down_out[columns, :] = (part * scale).astype(BF16)

    total = pair_sum(2 * y + xl)
    for d, e in offsets[::-1]:
        k = 2 * lax.rem(y - d + n, n) + lax.rem(xl + e, 2)
        pltpu.make_async_remote_copy(
            src_ref=y_send.at[k], dst_ref=y_recv.at[k], send_sem=send_sem.at[0],
            recv_sem=ig_y_sem.at[k], device_id=co_peer, device_id_type=MESH,
        ).wait_recv()
        total = total + y_recv[k].astype(F32)
    ig_out[...] = total.astype(BF16)

    for copy in sends:
        copy.wait_send()
    for k, copy in late:

        @pl.when(k != 2 * y + xl)
        def _():
            copy.wait_send()


def write_out(*refs):
    *pairs, sem = refs
    copies = []
    for src, dst in zip(pairs[:4], pairs[4:]):
        parts = 1 if src.shape[0] < 256 else 2
        rows = src.shape[0] // parts
        for k in range(parts):
            copies.append(
                pltpu.make_async_copy(
                    src.at[pl.ds(k * rows, rows)], dst.at[pl.ds(k * rows, rows)], sem.at[len(copies)]
                )
            )
            copies[-1].start()
    for copy in copies:
        copy.wait()


def on_device(n, tokens, upstream, gate_pre, up_pre, w_gate, w_up, w_down):
    d_block, f_block = w_gate.shape
    total = 32 * n
    blocks = 2 * n
    dma = pltpu.SemaphoreType.DMA
    hbm_spec = pl.BlockSpec(memory_space=pltpu.HBM)
    vmem_spec = pl.BlockSpec(memory_space=pltpu.VMEM)
    n_sends = 9 * n + 1
    grad_shapes = (
        jax.ShapeDtypeStruct((8, d_block), BF16),
        jax.ShapeDtypeStruct((d_block, f_block), BF16),
        jax.ShapeDtypeStruct((d_block, f_block), BF16),
        jax.ShapeDtypeStruct((f_block, d_block), BF16),
    )
    grads = pl.pallas_call(
        functools.partial(exchange, n, float(total) ** -0.5),
        name="exchange",
        out_shape=grad_shapes,
        in_specs=[hbm_spec] * 7,
        out_specs=[vmem_spec] * 4,
        scratch_shapes=[
            pltpu.VMEM((total, f_block), BF16),
            pltpu.VMEM((total, f_block), BF16),
            pltpu.VMEM((total, f_block), BF16),
            pltpu.VMEM((total, d_block), BF16),
            pltpu.VMEM((total, d_block), BF16),
            pltpu.VMEM((d_block, f_block), BF16),
            pltpu.VMEM((d_block, f_block), BF16),
            pltpu.VMEM((f_block, d_block), BF16),
            pltpu.VMEM((2, n, 2, 8, d_block), BF16),
            pltpu.VMEM((2, n, 2, 8, d_block), BF16),
            pltpu.VMEM((blocks, 2, 16, f_block), BF16),
            pltpu.VMEM((2, blocks, 8, f_block), F32),
            pltpu.VMEM((2, n, 8, f_block), BF16),
            pltpu.VMEM((2, n, 8, f_block), BF16),
            pltpu.VMEM((n, 2, 8, f_block), BF16),
            pltpu.VMEM((n, 2, 8, f_block), BF16),
            pltpu.VMEM((blocks, 16, f_block), BF16),
            pltpu.VMEM((blocks, 16, f_block), F32),
            pltpu.VMEM((blocks, 16, f_block), F32),
            pltpu.VMEM((blocks, 2, 8, d_block), F32),
            pltpu.VMEM((blocks, 8, d_block), F32),
            pltpu.VMEM((blocks, 8, d_block), BF16),
            pltpu.VMEM((blocks, 8, d_block), BF16),
            dma((7,)),
            dma((n_sends,)),
            dma((n,)), dma((n,)), dma((7,)),
            dma((n + 1,)), dma((2, n)), dma((n,)), dma((n,)), dma((2 * n,)), dma((2 * n,)), dma((n, 2)),
        ],
        compiler_params=pltpu.CompilerParams(
            collective_id=0, has_side_effects=True, vmem_limit_bytes=40 * 1024 * 1024
        ),
    )(*(
        pltpu.with_memory_space_constraint(a, pltpu.HBM)
        for a in (upstream, tokens, gate_pre, up_pre, w_gate, w_up, w_down)
    ))

    return pl.pallas_call(
        write_out,
        name="write_out",
        in_specs=[vmem_spec] * 4,
        out_specs=[pl.BlockSpec(memory_space=pl.ANY)] * 4,
        out_shape=grad_shapes,
        scratch_shapes=[dma((7,))],
        compiler_params=pltpu.CompilerParams(vmem_limit_bytes=16 * 1024 * 1024),
    )(*grads)


def solution(mesh):
    placed = (
        P("col", "row"),
        P("col", "row"),
        P("row", "col"),
        P("row", "col"),
        P("row", "col"),
        P("row", "col"),
        P("col", "row"),
    )
    return jax.shard_map(
        functools.partial(on_device, mesh.shape["row"] // 2),
        mesh=mesh,
        in_specs=placed,
        out_specs=(P("col", "row"), P("row", "col"), P("row", "col"), P("col", "row")),
        check_vma=False,
    )
```
